256 devices in a mesh: blk: 16 (over x_lo, z), rep: 16 (over x_hi, y, core).
Axes of the slice: x: 4 (x_hi: 2, x_lo: 2; x = x_hi * 2 + x_lo), y: 4, z: 8, core: 2. Of those that a mesh axis runs over, the one named last changes fastest.
Arguments:
- tokens: bfloat16 [131072, 2560], P(('blk', 'rep')), may hold values from -6 to 6
- cotangent: bfloat16 [131072, 2560], P(('blk', 'rep')), may hold values from -6 to 6
- gate_values: float32 [65536], P(('blk', 'rep')), may hold values from 0.2 to 1
- slot_rows: int32 [65536], P(('blk', 'rep')), may hold values from 0 to 511, as said below
- slot_counts: int32 [256], P(('blk', 'rep')), may hold values from 64 to 256, as said below
- gate_weight: bfloat16 [2560, 768], P(None, 'blk'), may hold values from -0.125 to 0.125
- up_weight: bfloat16 [2560, 768], P(None, 'blk'), may hold values from -0.125 to 0.125
- down_weight: bfloat16 [768, 2560], P('blk'), may hold values from -0.21875 to 0.21875
Outputs:
- layer_out: bfloat16 [131072, 2560], P(('blk', 'rep'))
- tokens_grad: bfloat16 [131072, 2560], P(('blk', 'rep'))
- gate_grad: float32 [65536], P(('blk', 'rep'))
- gate_weight_grad: bfloat16 [2560, 768], P(None, 'blk')
- up_weight_grad: bfloat16 [2560, 768], P(None, 'blk')
- down_weight_grad: bfloat16 [768, 2560], P('blk')
The draws below stay inside these ranges and needn't reach their ends.
Inputs may be any that keep to these rules, and one draw needn't show every extreme that they name: `slot_rows`: within one device the 256 slots name distinct resident rows. `slot_counts`: slots of a device at or beyond its count are padding. In every draw some device has all 256 slots live.
All inputs are finite; a program needn't handle non-finite values.
Results may differ from the reference program's by a relative error of at most 0.03.
Values may be sent and summed in bfloat16 or wider, within the bound.
No kernel may reach another device: no remote copies, remote signals or barrier semaphores. Data moves between devices by JAX's collectives and lax.ppermute only.
A program may use at most 128 MiB of HBM per device.

```python
import jax
import jax.numpy as jnp
from jax import lax

D = 2560
FFW = 768
CAP = 256
TOK_DEV = 512
TOKENS = 131072
SLOTS = 65536
N_BLK = 16
N_REP = 16
DEVICES = 256


def draw_slot_rows(key, part):
    key = jax.random.fold_in(key, 11)
    keys = jax.random.split(key, DEVICES)
    chosen = jax.vmap(lambda single: jax.random.permutation(single, TOK_DEV)[:CAP])(keys)
    return chosen.reshape(-1).astype(jnp.int32)


def draw_slot_counts(key, part):
    key = jax.random.fold_in(key, 23)
    first, second = jax.random.split(key)
    counts = jax.random.randint(first, (DEVICES,), CAP // 4, CAP + 1)
    fullest = jax.random.randint(second, (), 0, DEVICES)
    counts = jnp.where(jnp.arange(DEVICES) == fullest, CAP, counts)
    return counts.astype(jnp.int32)


def level_of(key, dims, cuts, least, top_value):
    def one(dim, shards_of):
        steps = jax.random.uniform(jax.random.fold_in(jax.random.fold_in(key, 6), dim), (shards_of,), jnp.float32, least / len(cuts), top_value / len(cuts))
        return jnp.repeat(jnp.exp(steps), dims[dim] // shards_of).reshape((-1,) + (1,) * (len(dims) - dim - 1))

    level = one(*cuts[0])
    for cut in cuts[1:]:
        level = level * one(*cut)
    return level


def noise(key, extent, spread, most, cuts=(), dtype=jnp.bfloat16):
    array = jax.random.normal(key, extent, jnp.float32) * spread
    if len(cuts) > 0:
        array = level_of(key, extent, cuts, -0.22, 0.18) * array
    return jnp.clip(array, min=-most, max=most).astype(dtype)


def setup_inputs(seed: int = 0) -> dict:
    streams_of = jax.random.split(jax.random.key(seed), 9)
    return {
        "tokens": noise(streams_of[0], (TOKENS, D), 1.0, 6.0, ((0, 256),)),
        "cotangent": noise(streams_of[1], (TOKENS, D), 1.0, 6.0, ((0, 256),)),
        "gate_values": jnp.clip(0.2 + 0.8 * jax.random.uniform(streams_of[2], (SLOTS,), jnp.float32) ** level_of(streams_of[2], (SLOTS,), ((0, 256),), -0.2, 0.2), 0.2, 1.0),
        "slot_rows": draw_slot_rows(jax.random.fold_in(streams_of[8], 71), 0),
        "slot_counts": draw_slot_counts(jax.random.fold_in(streams_of[8], 71), 0),
        "gate_weight": noise(streams_of[5], (D, FFW), D ** -0.5, 0.125, ((1, 16),)),
        "up_weight": noise(streams_of[6], (D, FFW), D ** -0.5, 0.125, ((1, 16),)),
        "down_weight": noise(streams_of[7], (FFW, D), FFW ** -0.5, 0.21875, ((0, 16),)),
    }


def device_pass(rows_in, grad_in, rows_idx, count, gates, gate_weight, up_weight, down_weight):
    live = (jnp.arange(CAP) < count).astype(jnp.float32)
    weighted = gates * live
    picked = jnp.take(rows_in, rows_idx, axis=0)
    picked_grad = jnp.take(grad_in, rows_idx, axis=0)
    scaled = (weighted[:, None] * picked_grad.astype(jnp.float32)).astype(jnp.bfloat16)
    gate_pre = jnp.dot(picked, gate_weight, preferred_element_type=jnp.float32)
    up_pre = jnp.dot(picked, up_weight, preferred_element_type=jnp.float32)
    sigma = jax.nn.sigmoid(gate_pre)
    active = gate_pre * sigma
    hidden = (active * up_pre).astype(jnp.bfloat16)
    expert_out = jnp.dot(hidden, down_weight, preferred_element_type=jnp.float32)
    out_rows = jnp.zeros((TOK_DEV, D), jnp.float32).at[rows_idx].add(weighted[:, None] * expert_out)
    gate_grad = live * jnp.sum(expert_out * picked_grad.astype(jnp.float32), axis=1)
    hidden_grad = jnp.dot(scaled, down_weight.T, preferred_element_type=jnp.float32)
    pre_gate = (hidden_grad * up_pre * (sigma + active * (1.0 - sigma))).astype(jnp.bfloat16)
    pre_up = (hidden_grad * active).astype(jnp.bfloat16)
    slot_grad = jnp.dot(pre_gate, gate_weight.T, preferred_element_type=jnp.float32)
    slot_grad = slot_grad + jnp.dot(pre_up, up_weight.T, preferred_element_type=jnp.float32)
    grad_rows = jnp.zeros((TOK_DEV, D), jnp.float32).at[rows_idx].add(slot_grad)
    term_gate = jnp.dot(picked.T, pre_gate, preferred_element_type=jnp.float32).astype(jnp.bfloat16)
    term_up = jnp.dot(picked.T, pre_up, preferred_element_type=jnp.float32).astype(jnp.bfloat16)
    term_down = jnp.dot(hidden.T, scaled, preferred_element_type=jnp.float32).astype(jnp.bfloat16)
    return (out_rows.astype(jnp.bfloat16), grad_rows.astype(jnp.bfloat16), gate_grad,
            term_gate, term_up, term_down)


def reference(tokens, cotangent, gate_values, slot_rows, slot_counts, gate_weight, up_weight, down_weight):
    tok = jnp.transpose(tokens.reshape(N_BLK, N_REP, TOK_DEV, D), (1, 0, 2, 3))
    cot = jnp.transpose(cotangent.reshape(N_BLK, N_REP, TOK_DEV, D), (1, 0, 2, 3))
    gvals = jnp.transpose(gate_values.reshape(N_BLK, N_REP, CAP), (1, 0, 2))
    rows = jnp.transpose(slot_rows.reshape(N_BLK, N_REP, CAP), (1, 0, 2))
    counts = jnp.transpose(slot_counts.reshape(N_BLK, N_REP), (1, 0))

    def inner(carry, item):
        rows_in, grad_in, rows_idx, count, gates = item
        out_rows, grad_rows, gate_grad, term_gate, term_up, term_down = device_pass(
            rows_in, grad_in, rows_idx, count, gates, gate_weight, up_weight, down_weight)
        carry = (carry[0] + term_gate.astype(jnp.float32), carry[1] + term_up.astype(jnp.float32),
                 carry[2] + term_down.astype(jnp.float32))
        return carry, (out_rows, grad_rows, gate_grad)

    def outer(carry, item):
        start = (jnp.zeros((D, FFW), jnp.float32), jnp.zeros((D, FFW), jnp.float32),
                 jnp.zeros((FFW, D), jnp.float32))
        group, results = lax.scan(inner, start, item)
        carry = tuple(c + g.astype(jnp.bfloat16).astype(jnp.float32) for c, g in zip(carry, group))
        return carry, results

    start = (jnp.zeros((D, FFW), jnp.float32), jnp.zeros((D, FFW), jnp.float32),
             jnp.zeros((FFW, D), jnp.float32))
    totals, results = lax.scan(outer, start, (tok, cot, rows, counts, gvals))
    out_rows, grad_rows, gate_grad = results
    layer_out = jnp.transpose(out_rows, (1, 0, 2, 3)).reshape(TOKENS, D)
    tokens_grad = jnp.transpose(grad_rows, (1, 0, 2, 3)).reshape(TOKENS, D)
    gate_grad = jnp.transpose(gate_grad, (1, 0, 2)).reshape(SLOTS)
    return (layer_out, tokens_grad, gate_grad, totals[0].astype(jnp.bfloat16),
            totals[1].astype(jnp.bfloat16), totals[2].astype(jnp.bfloat16))
```

```python
import itertools

import jax
import jax.numpy as jnp
from jax import lax
from jax.sharding import Mesh, PartitionSpec as P

NX, NY, NZ = 4, 4, 8
AXES = ("xl", "z", "xh", "y", "c")
ROWS = P(AXES)
SHARD = ("xl", "z")
PART = 16

F32 = jnp.float32
BF16 = jnp.bfloat16


def device_index(x, y, z, c):
    return ((((x % 2) * NZ + z) * 2 + x // 2) * NY + y) * 2 + c


def route(move):
    pairs = []
    for x, y, z, c in itertools.product(range(NX), range(NY), range(NZ), range(2)):
        target = move(x, y, z, c)
        if target is None:
            continue
        tx, ty, tz, tc = target
        pairs.append((device_index(x, y, z, c), device_index(tx % NX, ty % NY, tz % NZ, tc)))
    return pairs


Z_UP = route(lambda x, y, z, c: (x, y, z + 1, c))
Z_DOWN = route(lambda x, y, z, c: (x, y, z - 1, c))
Z_SPLIT = route(lambda x, y, z, c: (x, y, z + 1 - 2 * c, c))
Y_UP = route(lambda x, y, z, c: (x, y + 1, z, c))
Y_DOWN = route(lambda x, y, z, c: (x, y - 1, z, c))
Y_SPLIT = route(lambda x, y, z, c: (x, y + 1 - 2 * c, z, c))
X_UP = route(lambda x, y, z, c: (x + 1, y, z, c))
X_DOWN = route(lambda x, y, z, c: (x - 1, y, z, c))
X_SPLIT = route(lambda x, y, z, c: (x + 1 - 2 * c, y, z, c))
X_PAIR = route(lambda x, y, z, c: (x ^ 1, y, z, c))
X_PAIR_ODD = route(lambda x, y, z, c: (((x + 1) ^ 1) - 1, y, z, c))
Y_PAIR = route(lambda x, y, z, c: (x, y ^ 1, z, c))
Y_PAIR_ODD = route(lambda x, y, z, c: (x, ((y + 1) ^ 1) - 1, z, c))
CORE = route(lambda x, y, z, c: (x, y, z, 1 - c))
LEND_UP = route(lambda x, y, z, c: (x + 1, y, z, 1 - c) if c != x % 2 else None)
LEND_DOWN = route(lambda x, y, z, c: (x - 1, y, z, 1 - c) if c != x % 2 else None)


def send(block, pairs):
    return lax.ppermute(block, AXES, pairs)


def added(left, right):
    return (left.astype(F32) + right.astype(F32)).astype(BF16)


def columns(block, index, count):
    width = block.shape[-1] // count
    return lax.dynamic_slice_in_dim(block, (index % count) * width, width, block.ndim - 1)


def ring4_gather(block, core, up, down, split):
    below = send(block, up)
    above = send(block, down)
    across = send(jnp.where(core == 0, below, above), split)
    return block, below, above, across


def placed(blocks, index):
    own, below, above, across = blocks
    width = own.shape[-1]
    whole = jnp.zeros(own.shape[:-1] + (4 * width,), own.dtype)
    for shift, part in ((0, own), (3, below), (1, above), (2, across)):
        start = ((index + shift) % 4) * width
        whole = lax.dynamic_update_slice_in_dim(whole, part, start, own.ndim - 1)
    return whole


def ring4_reduce(block, index, core, up, down, split):
    first = send(columns(block, index + 2, 4), split)
    ahead = columns(block, index + 1, 4)
    behind = columns(block, index + 3, 4)
    ahead = jnp.where(core == 0, added(ahead, first), ahead)
    behind = jnp.where(core == 0, behind, added(behind, first))
    from_below = send(ahead, up)
    from_above = send(behind, down)
    own = columns(block, index, 4).astype(F32)
    return (own + from_below.astype(F32) + from_above.astype(F32)).astype(BF16)


def ring8_gather(block, core):
    blocks = [block]
    below, above = block, block
    for _ in range(3):
        below = send(below, Z_UP)
        above = send(above, Z_DOWN)
        blocks += [below, above]
    blocks.append(send(jnp.where(core == 0, below, above), Z_SPLIT))
    return blocks


def ring8_reduce(blocks, core):
    own, below1, above1, below2, above2, below3, above3, far = blocks
    first = send(far, Z_SPLIT)
    above3 = jnp.where(core == 0, added(above3, first), above3)
    below3 = jnp.where(core == 0, below3, added(below3, first))
    above2 = added(above2, send(above3, Z_UP))
    below2 = added(below2, send(below3, Z_DOWN))
    above1 = added(above1, send(above2, Z_UP))
    below1 = added(below1, send(below2, Z_DOWN))
    from_below = send(above1, Z_UP)
    from_above = send(below1, Z_DOWN)
    return (own.astype(F32) + from_below.astype(F32) + from_above.astype(F32)).astype(BF16)


def pair_sum(block, first, second):
    block = added(block, send(block, first))
    return added(block, send(block, second))


def inner_rows(left, right):
    return lax.dot_general(left, right, (((0,), (0,)), ((), ())), preferred_element_type=F32)


def inner_cols(left, right):
    return lax.dot_general(left, right, (((1,), (1,)), ((), ())), preferred_element_type=F32)


def matrix(whole, index):
    width = whole.shape[-1]
    return whole.reshape(NZ, 3, PART, width)[:, index].reshape(NZ * PART, width)


def stacked(parts):
    width = parts[0].shape[-1]
    return jnp.stack([p.reshape(NZ, PART, width) for p in parts], 1).reshape(NZ * 3 * PART, width)


def local(
    tokens, cotangent, gate_values, slot_rows, slot_counts, gate_weight, up_weight, down_weight
):
    cap = slot_rows.shape[0]
    width = tokens.shape[1]
    xl, y, core = lax.axis_index("xl"), lax.axis_index("y"), lax.axis_index("c")
    x = 2 * lax.axis_index("xh") + xl
    mine = core == xl

    mats = (gate_weight.T, up_weight.T, down_weight)
    part_z, part_y, part_x = (
        jnp.concatenate([m[i * PART : (i + 1) * PART] for m in mats], 0) for i in range(3)
    )
    quarter_y = columns(part_y, y, 4)
    lent = send(jnp.concatenate([quarter_y, columns(part_x, x + 1, 4)], 1), LEND_UP)
    small = jnp.concatenate([quarter_y, columns(part_x, x, 4)], 1)
    small = jnp.where(mine, small, lent)
    large = jnp.where(mine, part_z, send(part_z, LEND_DOWN))

    whole_z = lax.all_gather(large, "z", axis=0, tiled=True)

    blocks = ring8_gather(small, core)
    quarter = width // 4
    along_y = jnp.concatenate([b[:, :quarter] for b in blocks], 0)
    along_x = jnp.concatenate([b[:, quarter:] for b in blocks], 0)
    whole_y = placed(ring4_gather(along_y, core, Y_UP, Y_DOWN, Y_SPLIT), y)
    whole_x = placed(ring4_gather(along_x, core, X_UP, X_DOWN, X_SPLIT), x)

    live = (lax.iota(jnp.int32, cap) < slot_counts[0]).astype(F32)
    weighted = gate_values * live
    chosen = (slot_rows[:, None] == lax.broadcasted_iota(jnp.int32, (cap, tokens.shape[0]), 1))
    chosen = chosen.astype(BF16)
    picked = jnp.dot(chosen, tokens, preferred_element_type=F32).astype(BF16)
    picked_grad = jnp.dot(chosen, cotangent, preferred_element_type=F32).astype(BF16)
    other = send(jnp.concatenate([picked, picked_grad], 0), CORE)
    rows = jnp.concatenate([picked, other[:cap]], 0)
    grads = jnp.concatenate([picked_grad, other[cap:]], 0)
    weight = jnp.concatenate([weighted, send(weighted, CORE)], 0)[:, None]

    wholes = (whole_z, whole_y, whole_x)
    w_gate, w_up, w_down = (
        jnp.concatenate([matrix(whole, i) for whole in wholes], 0) for i in range(3)
    )
    gate_pre = inner_cols(rows, w_gate)
    up_pre = inner_cols(rows, w_up)
    down_grad = inner_cols(grads, w_down)
    sigma = jax.nn.sigmoid(gate_pre)
    active = gate_pre * sigma
    hidden = active * up_pre
    gate_part = jnp.sum(hidden * down_grad, axis=1)
    hidden_weighted = (weight * hidden).astype(BF16)
    hidden_grad = weight * down_grad
    pre_gate = (hidden_grad * up_pre * (sigma + active * (1.0 - sigma))).astype(BF16)
    pre_up = (hidden_grad * active).astype(BF16)

    terms = (inner_rows(pre_gate, rows), inner_rows(pre_up, rows), inner_rows(hidden_weighted, grads))
    terms = [t.astype(BF16) for t in terms]
    group = NZ * PART
    term_z, term_y, term_x = (
        stacked([t[i * group : (i + 1) * group] for t in terms]) for i in range(3)
    )
    sum_z = lax.psum_scatter(term_z, "z", scatter_dimension=0, tiled=True)
    sum_y = ring4_reduce(term_y, y, core, Y_UP, Y_DOWN, Y_SPLIT)
    sum_x = ring4_reduce(term_x, x, core, X_UP, X_DOWN, X_SPLIT)
    sums = jnp.concatenate([sum_y, sum_x], 1).reshape(NZ, 3 * PART, 2 * quarter)
    sums = ring8_reduce([sums[i] for i in range(NZ)], core)

    expert_part = jnp.dot(hidden_weighted, w_down, preferred_element_type=F32)
    slot_part = jnp.dot(pre_gate, w_gate, preferred_element_type=F32)
    slot_part = slot_part + jnp.dot(pre_up, w_up, preferred_element_type=F32)
    back = jnp.concatenate([expert_part[cap:].astype(BF16), slot_part[cap:].astype(BF16)], 0)
    back = send(back, CORE)
    expert_out = added(expert_part[:cap], back[:cap])
    slot_grad = added(slot_part[:cap], back[cap:])
    gate_grad = live * (gate_part[:cap] + send(gate_part[cap:], CORE))
    layer_out = inner_rows(chosen, expert_out).astype(BF16)
    tokens_grad = inner_rows(chosen, slot_grad).astype(BF16)

    end_z = ring4_reduce(sum_z, y, core, Y_UP, Y_DOWN, Y_SPLIT)
    end_zy = pair_sum(jnp.concatenate([end_z, sums[:, :quarter]], 1), X_PAIR, X_PAIR_ODD)
    end_x = pair_sum(sums[:, quarter:], Y_PAIR, Y_PAIR_ODD)
    parts_zy = ring4_gather(end_zy, core, Y_UP, Y_DOWN, Y_SPLIT)
    full_z = placed([b[:, :quarter] for b in parts_zy], y)
    full_y = placed([b[:, quarter:] for b in parts_zy], y)
    full_x = placed(ring4_gather(end_x, core, X_UP, X_DOWN, X_SPLIT), x)
    fulls = (full_z, full_y, full_x)
    shard = jnp.concatenate(
        [full[i * PART : (i + 1) * PART] for i in range(3) for full in fulls], 0
    )
    shard = jnp.where(mine, shard, send(shard, CORE))
    units = 3 * PART
    return (
        layer_out,
        tokens_grad,
        gate_grad,
        shard[:units].T,
        shard[units : 2 * units].T,
        shard[2 * units :],
    )


def solution(mesh):
    grid = Mesh(mesh.devices.reshape(2, NZ, 2, NY, 2), AXES)
    rows = P(AXES, None)
    vector = P(AXES)
    weights = (P(None, SHARD), P(None, SHARD), P(SHARD, None))
    return jax.shard_map(
        local,
        mesh=grid,
        in_specs=(rows, rows, vector, vector, vector) + weights,
        out_specs=(rows, rows, vector) + weights,
        check_vma=False,
    )
```

```python
import itertools

import jax
import jax.numpy as jnp
from jax import lax
from jax.sharding import Mesh, PartitionSpec as P

NX, NY, NZ = 4, 4, 8
AXES = ("xl", "z", "xh", "y", "c")
ROWS = P(AXES)
SHARD = ("xl", "z")
F32 = jnp.float32
BF16 = jnp.bfloat16


def device_index(x, y, z, c):
    return ((((x % 2) * NZ + z) * 2 + x // 2) * NY + y) * 2 + c


def route(move):
    pairs = []
    for x, y, z, c in itertools.product(range(NX), range(NY), range(NZ), range(2)):
        target = move(x, y, z, c)
        if target is None:
            continue
        tx, ty, tz, tc = target
        pairs.append((device_index(x, y, z, c), device_index(tx % NX, ty % NY, tz % NZ, tc)))
    return pairs


Z_UP = route(lambda x, y, z, c: (x, y, z + 1, c))
Z_DOWN = route(lambda x, y, z, c: (x, y, z - 1, c))
Z_SPLIT = route(lambda x, y, z, c: (x, y, z + 1 - 2 * c, c))
Y_UP = route(lambda x, y, z, c: (x, y + 1, z, c))
Y_DOWN = route(lambda x, y, z, c: (x, y - 1, z, c))
Y_SPLIT = route(lambda x, y, z, c: (x, y + 1 - 2 * c, z, c))
X_UP = route(lambda x, y, z, c: (x + 1, y, z, c))
X_DOWN = route(lambda x, y, z, c: (x - 1, y, z, c))
X_SPLIT = route(lambda x, y, z, c: (x + 1 - 2 * c, y, z, c))
X_ACROSS = route(lambda x, y, z, c: (x + 2, y, z, c))
CORE = route(lambda x, y, z, c: (x, y, z, 1 - c))

def send(block, pairs):
    return lax.ppermute(block, AXES, pairs)


def added(left, right):
    return (left.astype(F32) + right.astype(F32)).astype(BF16)


def columns(block, index, count):
    width = block.shape[-1] // count
    return lax.dynamic_slice_in_dim(block, (index % count) * width, width, block.ndim - 1)


def ring4_gather(block, core, up, down, split):
    below = send(block, up)
    above = send(block, down)
    across = send(jnp.where(core == 0, below, above), split)
    return block, below, above, across


def placed(blocks, index):
    own, below, above, across = blocks
    width = own.shape[-1]
    whole = jnp.zeros(own.shape[:-1] + (4 * width,), own.dtype)
    for shift, part in ((0, own), (3, below), (1, above), (2, across)):
        start = ((index + shift) % 4) * width
        whole = lax.dynamic_update_slice_in_dim(whole, part, start, own.ndim - 1)
    return whole


def ring4_reduce(block, index, core, up, down, split):
    first = send(columns(block, index + 2, 4), split)
    ahead = columns(block, index + 1, 4)
    behind = columns(block, index + 3, 4)
    ahead = jnp.where(core == 0, added(ahead, first), ahead)
    behind = jnp.where(core == 0, behind, added(behind, first))
    from_below = send(ahead, up)
    from_above = send(behind, down)
    own = columns(block, index, 4).astype(F32)
    return (own + from_below.astype(F32) + from_above.astype(F32)).astype(BF16)


def ring8_gather(block, core):
    blocks = [block]
    below, above = block, block
    for _ in range(3):
        below = send(below, Z_UP)
        above = send(above, Z_DOWN)
        blocks += [below, above]
    blocks.append(send(jnp.where(core == 0, below, above), Z_SPLIT))
    return blocks


def ring8_reduce(blocks, core):
    own, below1, above1, below2, above2, below3, above3, far = blocks
    first = send(far, Z_SPLIT)
    above3 = jnp.where(core == 0, added(above3, first), above3)
    below3 = jnp.where(core == 0, below3, added(below3, first))
    above2 = added(above2, send(above3, Z_UP))
    below2 = added(below2, send(below3, Z_DOWN))
    above1 = added(above1, send(above2, Z_UP))
    below1 = added(below1, send(below2, Z_DOWN))
    from_below = send(above1, Z_UP)
    from_above = send(below1, Z_DOWN)
    return (own.astype(F32) + from_below.astype(F32) + from_above.astype(F32)).astype(BF16)


def inner_rows(left, right):
    return lax.dot_general(left, right, (((0,), (0,)), ((), ())), preferred_element_type=F32)


def inner_cols(left, right):
    return lax.dot_general(left, right, (((1,), (1,)), ((), ())), preferred_element_type=F32)


def split_rows(block, count):
    rows = block.shape[0] // count
    return [block[i * rows : (i + 1) * rows] for i in range(count)]


def by_matrix(pieces):
    width = pieces[0].shape[-1]
    whole = jnp.concatenate([p.reshape(3, -1, width) for p in pieces], 1)
    return whole[0], whole[1], whole[2]


def by_piece(terms, count):
    parts = [split_rows(term, count) for term in terms]
    return [jnp.concatenate([part[i] for part in parts], 0) for i in range(count)]


def forward(rows, grads, weight, pieces):
    w_gate, w_up, w_down = by_matrix(pieces)
    gate_pre = inner_cols(rows, w_gate)
    up_pre = inner_cols(rows, w_up)
    down_grad = inner_cols(grads, w_down)
    sigma = jax.nn.sigmoid(gate_pre)
    active = gate_pre * sigma
    hidden = active * up_pre
    gate_part = jnp.sum(hidden * down_grad, axis=1)
    hidden_weighted = (weight * hidden).astype(BF16)
    hidden_grad = weight * down_grad
    pre_gate = (hidden_grad * up_pre * (sigma + active * (1.0 - sigma))).astype(BF16)
    pre_up = (hidden_grad * active).astype(BF16)
    return (w_gate, w_up, w_down), (pre_gate, pre_up, hidden_weighted), gate_part


def weight_terms(rows, grads, units, count):
    pre_gate, pre_up, hidden_weighted = units
    terms = (inner_rows(pre_gate, rows), inner_rows(pre_up, rows), inner_rows(hidden_weighted, grads))
    return by_piece([t.astype(BF16) for t in terms], count)


def row_terms(units, mats):
    pre_gate, pre_up, hidden_weighted = units
    w_gate, w_up, w_down = mats
    expert_part = jnp.dot(hidden_weighted, w_down, preferred_element_type=F32)
    slot_part = jnp.dot(pre_gate, w_gate, preferred_element_type=F32)
    return expert_part, slot_part + jnp.dot(pre_up, w_up, preferred_element_type=F32)


def beside(pieces):
    return split_rows(send(jnp.concatenate(pieces, 0), X_SPLIT), len(pieces))


def local(
    tokens, cotangent, gate_values, slot_rows, slot_counts, gate_weight, up_weight, down_weight
):
    cap = slot_rows.shape[0]
    y, core = lax.axis_index("y"), lax.axis_index("c")
    half = down_weight.shape[0] // 2

    mats = (gate_weight.T, up_weight.T, down_weight)
    piece = jnp.concatenate([lax.dynamic_slice_in_dim(m, core * half, half, 0) for m in mats], 0)
    ring = ring8_gather(piece, core)
    near = ring[:5] + beside(ring[:1]) + beside(ring[1:3]) + beside(ring[3:5])
    far = ring[5:] + beside(ring[5:7]) + beside(ring[7:])

    live = (lax.iota(jnp.int32, cap) < slot_counts[0]).astype(F32)
    weighted = gate_values * live
    n_rows = tokens.shape[0]
    chosen = slot_rows[:, None] == lax.broadcasted_iota(jnp.int32, (cap, n_rows), 1)
    chosen = chosen.astype(BF16)
    picked = jnp.dot(chosen, tokens, preferred_element_type=F32).astype(BF16)
    picked_grad = jnp.dot(chosen, cotangent, preferred_element_type=F32).astype(BF16)
    other = send(jnp.concatenate([picked, picked_grad], 0), CORE)
    rows = jnp.concatenate([picked, other[:cap]], 0)
    grads = jnp.concatenate([picked_grad, other[cap:]], 0)
    weight = jnp.concatenate([weighted, send(weighted, CORE)], 0)[:, None]

    near_mats, near_units, near_gate = forward(rows, grads, weight, near)
    far_mats, far_units, far_gate = forward(rows, grads, weight, far)

    far_terms = weight_terms(rows, grads, far_units, len(far))
    own = [None] * 8
    own[7] = added(far_terms[2], send(far_terms[5], X_SPLIT))
    back = split_rows(send(jnp.concatenate(far_terms[3:5], 0), X_SPLIT), 2)
    own[5], own[6] = added(far_terms[0], back[0]), added(far_terms[1], back[1])
    near_terms = weight_terms(rows, grads, near_units, len(near))
    for i in (3, 1):
        back = split_rows(send(jnp.concatenate(near_terms[5 + i : 7 + i], 0), X_SPLIT), 2)
        own[i], own[i + 1] = added(near_terms[i], back[0]), added(near_terms[i + 1], back[1])
    own[0] = added(near_terms[0], send(near_terms[5], X_SPLIT))
    total = ring8_reduce(own, core)

    near_rows = row_terms(near_units, near_mats)
    far_rows = row_terms(far_units, far_mats)
    expert_part, slot_part = (a + b for a, b in zip(near_rows, far_rows))
    gate_part = near_gate + far_gate
    back = jnp.concatenate([expert_part[cap:].astype(BF16), slot_part[cap:].astype(BF16)], 0)
    back = send(back, CORE)
    expert_out = added(expert_part[:cap], back[:cap])
    slot_grad = added(slot_part[:cap], back[cap:])
    gate_grad = live * (gate_part[:cap] + send(gate_part[cap:], CORE))
    placing = slot_rows[None, :] == lax.broadcasted_iota(jnp.int32, (n_rows, cap), 0)
    placing = placing.astype(BF16)
    layer_out = jnp.dot(placing, expert_out, preferred_element_type=F32).astype(BF16)
    tokens_grad = jnp.dot(placing, slot_grad, preferred_element_type=F32).astype(BF16)
    total, layer_out, tokens_grad, gate_grad = lax.optimization_barrier(
        (total, layer_out, tokens_grad, gate_grad)
    )

    quarter = ring4_reduce(total, y, core, Y_UP, Y_DOWN, Y_SPLIT)
    quarter = added(quarter, send(quarter, X_ACROSS))
    total = placed(ring4_gather(quarter, core, Y_UP, Y_DOWN, Y_SPLIT), y)
    swapped = send(total, CORE)
    first = jnp.where(core == 0, total, swapped)
    second = jnp.where(core == 0, swapped, total)
    g, u, d = (
        jnp.concatenate([first[i * half : (i + 1) * half], second[i * half : (i + 1) * half]], 0)
        for i in range(3)
    )
    return layer_out, tokens_grad, gate_grad, g.T, u.T, d


def solution(mesh):
    grid = Mesh(mesh.devices.reshape(2, NZ, 2, NY, 2), AXES)
    rows = P(AXES, None)
    vector = P(AXES)
    weights = (P(None, SHARD), P(None, SHARD), P(SHARD, None))
    return jax.shard_map(
        local,
        mesh=grid,
        in_specs=(rows, rows, vector, vector, vector) + weights,
        out_specs=(rows, rows, vector) + weights,
        check_vma=False,
    )
```

```python
import itertools

import jax
import jax.numpy as jnp
from jax import lax
from jax.sharding import Mesh, PartitionSpec as P

NX, NY, NZ = 4, 4, 8
AXES = ("xl", "z", "xh", "y", "c")
ROWS = P(AXES)
SHARD = ("xl", "z")
F32 = jnp.float32
BF16 = jnp.bfloat16


def device_index(x, y, z, c):
    return ((((x % 2) * NZ + z) * 2 + x // 2) * NY + y) * 2 + c


def route(move):
    pairs = []
    for x, y, z, c in itertools.product(range(NX), range(NY), range(NZ), range(2)):
        target = move(x, y, z, c)
        if target is None:
            continue
        tx, ty, tz, tc = target
        pairs.append((device_index(x, y, z, c), device_index(tx % NX, ty % NY, tz % NZ, tc)))
    return pairs


Z_OUT = route(lambda x, y, z, c: (x, y, z + 1 - 2 * c, c))
Z_BACK = route(lambda x, y, z, c: (x, y, z - 1 + 2 * c, c))
X_OUT = route(lambda x, y, z, c: (x + 1 - 2 * c, y, z, c))
X_BACK = route(lambda x, y, z, c: (x - 1 + 2 * c, y, z, c))
X_ACROSS = route(lambda x, y, z, c: (x + 2, y, z, c))
Y_UP = route(lambda x, y, z, c: (x, y + 1, z, c))
Y_DOWN = route(lambda x, y, z, c: (x, y - 1, z, c))
Y_TWO = route(lambda x, y, z, c: (x, y + 2, z, c))
CORE = route(lambda x, y, z, c: (x, y, z, 1 - c))


def send(block, pairs):
    return lax.ppermute(block, AXES, pairs)


def added(left, right):
    return (left.astype(F32) + right.astype(F32)).astype(BF16)


def columns(block, index, count):
    width = block.shape[-1] // count
    return lax.dynamic_slice_in_dim(block, (index % count) * width, width, block.ndim - 1)


def y_gather(block):
    return block, send(block, Y_UP), send(block, Y_DOWN), send(block, Y_TWO)


def placed(blocks, index):
    own, below, above, across = blocks
    width = own.shape[-1]
    whole = jnp.zeros(own.shape[:-1] + (4 * width,), own.dtype)
    for shift, part in ((0, own), (3, below), (1, above), (2, across)):
        start = ((index + shift) % 4) * width
        whole = lax.dynamic_update_slice_in_dim(whole, part, start, own.ndim - 1)
    return whole


def y_reduce(block, y, other):
    routes = ((1, Y_UP), (3, Y_DOWN), (2, Y_TWO))
    parts = [send(columns(block, y + shift, 4), pairs) for shift, pairs in routes]
    parts, other = lax.optimization_barrier((parts, other))
    total = columns(block, y, 4).astype(F32)
    for part in parts:
        total = total + part.astype(F32)
    return total.astype(BF16), other


def ring8_gather(block):
    blocks = [block]
    behind, ahead = block, block
    for _ in range(3):
        behind = send(behind, Z_OUT)
        ahead = send(ahead, Z_BACK)
        blocks += [behind, ahead]
    return blocks + [send(behind, Z_OUT)]


def inner_rows(left, right):
    return lax.dot_general(left, right, (((0,), (0,)), ((), ())), preferred_element_type=F32)


def inner_cols(left, right):
    return lax.dot_general(left, right, (((1,), (1,)), ((), ())), preferred_element_type=F32)


def split_rows(block, count):
    rows = block.shape[0] // count
    return [block[i * rows : (i + 1) * rows] for i in range(count)]


def by_matrix(pieces):
    width = pieces[0].shape[-1]
    whole = jnp.concatenate([p.reshape(3, -1, width) for p in pieces], 1)
    return whole[0], whole[1], whole[2]


def by_piece(terms, count):
    parts = [split_rows(term, count) for term in terms]
    return [jnp.concatenate([part[i] for part in parts], 0) for i in range(count)]


def forward(rows, scaled, mats):
    w_gate, w_up, w_down = mats
    gate_pre = inner_cols(rows, w_gate)
    up_pre = inner_cols(rows, w_up)
    hidden_grad = inner_cols(scaled, w_down)
    sigma = jax.nn.sigmoid(gate_pre)
    active = gate_pre * sigma
    hidden = (active * up_pre).astype(BF16)
    pre_gate = (hidden_grad * up_pre * (sigma + active * (1.0 - sigma))).astype(BF16)
    pre_up = (hidden_grad * active).astype(BF16)
    return pre_gate, pre_up, hidden


def row_terms(units, mats):
    pre_gate, pre_up, hidden = units
    w_gate, w_up, w_down = mats
    expert_part = jnp.dot(hidden, w_down, preferred_element_type=F32)
    slot_part = jnp.dot(pre_gate, w_gate, preferred_element_type=F32)
    return expert_part, slot_part + jnp.dot(pre_up, w_up, preferred_element_type=F32)


def local(
    tokens, cotangent, gate_values, slot_rows, slot_counts, gate_weight, up_weight, down_weight
):
    cap = slot_rows.shape[0]
    n_rows = tokens.shape[0]
    part = cap // 2
    y, core = lax.axis_index("y"), lax.axis_index("c")
    half = down_weight.shape[0] // 2

    mats = (gate_weight.T, up_weight.T, down_weight)
    piece = jnp.concatenate([lax.dynamic_slice_in_dim(m, core * half, half, 0) for m in mats], 0)
    ring = ring8_gather(piece)

    live = (lax.iota(jnp.int32, cap) < slot_counts[0]).astype(F32)
    weighted = (gate_values * live)[:, None]
    chosen = slot_rows[:, None] == lax.broadcasted_iota(jnp.int32, (cap, n_rows), 1)
    chosen = chosen.astype(BF16)
    picked = jnp.dot(chosen, tokens, preferred_element_type=F32).astype(BF16)
    picked_grad = jnp.dot(chosen, cotangent, preferred_element_type=F32)
    scaled = (weighted * picked_grad).astype(BF16)
    picked_grad = picked_grad.astype(BF16)

    other = send(jnp.concatenate([picked, scaled], 0), CORE)
    lent = send(jnp.concatenate([picked[:part], scaled[:part]], 0), X_OUT)
    lent_back = send(jnp.concatenate([picked[part:], scaled[part:]], 0), X_BACK)
    guests = (lent, lent_back, send(lent, CORE), send(lent_back, CORE))
    rows = (
        jnp.concatenate([picked, other[:cap]], 0),
        jnp.concatenate([guest[:part] for guest in guests], 0),
    )
    grads = (
        jnp.concatenate([scaled, other[cap:]], 0),
        jnp.concatenate([guest[part:] for guest in guests], 0),
    )

    mats = by_matrix(ring)
    units = [forward(r, g, mats) for r, g in zip(rows, grads)]
    guest_parts = [split_rows(t, 4) for t in row_terms(units[1], mats)]
    guest_other = jnp.concatenate([p[i] for p in guest_parts for i in (2, 1)], 0).astype(BF16)
    guest_other, units = lax.optimization_barrier((guest_other, units))
    guest_own = jnp.concatenate([p[i] for p in guest_parts for i in (0, 3)], 0)
    guest_out = added(guest_own, send(guest_other, CORE))
    sides = ((0, rows), (1, rows), (2, grads))
    terms = [
        (inner_rows(units[0][i], side[0]) + inner_rows(units[1][i], side[1])).astype(BF16)
        for i, side in sides
    ]
    home_parts = [split_rows(t, 4) for t in row_terms(units[0], mats)]

    own, behind1, ahead1, behind2, ahead2, behind3, ahead3, far = by_piece(terms, len(ring))
    ahead3 = added(ahead3, send(far, Z_OUT))
    behind2 = added(behind2, send(behind3, Z_BACK))
    ahead3, behind2, guest_out = lax.optimization_barrier((ahead3, behind2, guest_out))
    returned = send(guest_out, X_BACK)
    ahead2 = added(ahead2, send(ahead3, Z_OUT))
    behind1 = added(behind1, send(behind2, Z_BACK))
    ahead1 = added(ahead1, send(ahead2, Z_OUT))
    total = own.astype(F32) + send(behind1, Z_BACK).astype(F32) + send(ahead1, Z_OUT).astype(F32)
    total = total.astype(BF16)
    quarter, returned = y_reduce(total, y, returned)

    results, message = [], []
    for part, back in zip(home_parts, (returned[:cap], returned[cap:])):
        mine, others = split_rows(back.astype(F32), 2)
        results.append(jnp.concatenate([part[0] + mine, part[1]], 0))
        message += [part[2], part[3] + others]
    message = send(jnp.concatenate(message, 0).astype(BF16), CORE)
    quarter = added(quarter, send(quarter, X_ACROSS))
    quarter, message = lax.optimization_barrier((quarter, message))
    total = placed(y_gather(quarter), y)
    expert_out = results[0] + message[:cap].astype(F32)
    slot_grad = results[1] + message[cap:].astype(F32)
    gate_grad = live * jnp.sum(expert_out * picked_grad.astype(F32), axis=1)
    placing = slot_rows[None, :] == lax.broadcasted_iota(jnp.int32, (n_rows, cap), 0)
    placing = placing.astype(BF16)
    weighted_out = (weighted * expert_out).astype(BF16)
    layer_out = jnp.dot(placing, weighted_out, preferred_element_type=F32).astype(BF16)
    tokens_grad = jnp.dot(placing, slot_grad.astype(BF16), preferred_element_type=F32).astype(BF16)
    total, layer_out, tokens_grad, gate_grad = lax.optimization_barrier(
        (total, layer_out, tokens_grad, gate_grad)
    )
    swapped = send(total, CORE)
    first = jnp.where(core == 0, total, swapped)
    second = jnp.where(core == 0, swapped, total)
    g, u, d = (
        jnp.concatenate([first[i * half : (i + 1) * half], second[i * half : (i + 1) * half]], 0)
        for i in range(3)
    )
    return layer_out, tokens_grad, gate_grad, g.T, u.T, d


def solution(mesh):
    grid = Mesh(mesh.devices.reshape(2, NZ, 2, NY, 2), AXES)
    rows = P(AXES, None)
    vector = P(AXES)
    weights = (P(None, SHARD), P(None, SHARD), P(SHARD, None))
    return jax.shard_map(
        local,
        mesh=grid,
        in_specs=(rows, rows, vector, vector, vector) + weights,
        out_specs=(rows, rows, vector) + weights,
        check_vma=False,
    )
```

```python
import itertools

import jax
import jax.numpy as jnp
from jax import lax
from jax.sharding import Mesh, PartitionSpec as P

NX, NY, NZ = 4, 4, 8
AXES = ("xl", "z", "xh", "y", "c")
ROWS = P(AXES)
SHARD = ("xl", "z")
F32 = jnp.float32
BF16 = jnp.bfloat16


def device_index(x, y, z, c):
    return ((((x % 2) * NZ + z) * 2 + x // 2) * NY + y) * 2 + c


def route(move):
    pairs = []
    for x, y, z, c in itertools.product(range(NX), range(NY), range(NZ), range(2)):
        target = move(x, y, z, c)
        if target is None:
            continue
        tx, ty, tz, tc = target
        pairs.append((device_index(x, y, z, c), device_index(tx % NX, ty % NY, tz % NZ, tc)))
    return pairs


Z_OUT = route(lambda x, y, z, c: (x, y, z + 1 - 2 * c, c))
Z_BACK = route(lambda x, y, z, c: (x, y, z - 1 + 2 * c, c))
X_OUT = route(lambda x, y, z, c: (x + 1 - 2 * c, y, z, c))
X_BACK = route(lambda x, y, z, c: (x - 1 + 2 * c, y, z, c))
X_ACROSS = route(lambda x, y, z, c: (x + 2, y, z, c))
Y_UP = route(lambda x, y, z, c: (x, y + 1, z, c))
Y_DOWN = route(lambda x, y, z, c: (x, y - 1, z, c))
Y_TWO = route(lambda x, y, z, c: (x, y + 2, z, c))
CORE = route(lambda x, y, z, c: (x, y, z, 1 - c))


def send(block, pairs):
    return lax.ppermute(block, AXES, pairs)


def added(left, right):
    return (left.astype(F32) + right.astype(F32)).astype(BF16)


def columns(block, index, count):
    width = block.shape[-1] // count
    return lax.dynamic_slice_in_dim(block, (index % count) * width, width, block.ndim - 1)


def y_gather(block):
    return block, send(block, Y_UP), send(block, Y_DOWN), send(block, Y_TWO)


def placed(blocks, index):
    own, below, above, across = blocks
    width = own.shape[-1]
    whole = jnp.zeros(own.shape[:-1] + (4 * width,), own.dtype)
    for shift, part in ((0, own), (3, below), (1, above), (2, across)):
        start = ((index + shift) % 4) * width
        whole = lax.dynamic_update_slice_in_dim(whole, part, start, own.ndim - 1)
    return whole


def y_reduce(block, y, other):
    routes = ((1, Y_UP), (3, Y_DOWN), (2, Y_TWO))
    parts = [send(columns(block, y + shift, 4), pairs) for shift, pairs in routes]
    parts, other = lax.optimization_barrier((parts, other))
    total = columns(block, y, 4).astype(F32)
    for part in parts:
        total = total + part.astype(F32)
    return total.astype(BF16), other


def ring8_gather(block):
    blocks = [block]
    behind, ahead = block, block
    for _ in range(3):
        behind = send(behind, Z_OUT)
        ahead = send(ahead, Z_BACK)
        blocks += [behind, ahead]
    return blocks + [send(behind, Z_OUT)]


def inner_rows(left, right):
    return lax.dot_general(left, right, (((0,), (0,)), ((), ())), preferred_element_type=F32)


def inner_cols(left, right):
    return lax.dot_general(left, right, (((1,), (1,)), ((), ())), preferred_element_type=F32)


def split_rows(block, count):
    rows = block.shape[0] // count
    return [block[i * rows : (i + 1) * rows] for i in range(count)]


def by_matrix(pieces):
    width = pieces[0].shape[-1]
    whole = jnp.concatenate([p.reshape(3, -1, width) for p in pieces], 1)
    return whole[0], whole[1], whole[2]


def by_piece(terms, count):
    parts = [split_rows(term, count) for term in terms]
    return [jnp.concatenate([part[i] for part in parts], 0) for i in range(count)]


def forward(rows, scaled, mats):
    w_gate, w_up, w_down = mats
    gate_pre = inner_cols(rows, w_gate)
    up_pre = inner_cols(rows, w_up)
    hidden_grad = inner_cols(scaled, w_down)
    sigma = jax.nn.sigmoid(gate_pre)
    active = gate_pre * sigma
    hidden = (active * up_pre).astype(BF16)
    pre_gate = (hidden_grad * up_pre * (sigma + active * (1.0 - sigma))).astype(BF16)
    pre_up = (hidden_grad * active).astype(BF16)
    return pre_gate, pre_up, hidden


def row_terms(units, mats):
    pre_gate, pre_up, hidden = units
    w_gate, w_up, w_down = mats
    expert_part = jnp.dot(hidden, w_down, preferred_element_type=F32)
    slot_part = jnp.dot(pre_gate, w_gate, preferred_element_type=F32)
    return expert_part, slot_part + jnp.dot(pre_up, w_up, preferred_element_type=F32)


def local(
    tokens, cotangent, gate_values, slot_rows, slot_counts, gate_weight, up_weight, down_weight
):
    cap = slot_rows.shape[0]
    n_rows = tokens.shape[0]
    part = cap // 2
    y, core = lax.axis_index("y"), lax.axis_index("c")
    half = down_weight.shape[0] // 2

    mats = (gate_weight.T, up_weight.T, down_weight)
    piece = jnp.concatenate([lax.dynamic_slice_in_dim(m, core * half, half, 0) for m in mats], 0)
    ring = ring8_gather(piece)

    live = (lax.iota(jnp.int32, cap) < slot_counts[0]).astype(F32)
    weighted = (gate_values * live)[:, None]
    chosen = slot_rows[:, None] == lax.broadcasted_iota(jnp.int32, (cap, n_rows), 1)
    placing = slot_rows[None, :] == lax.broadcasted_iota(jnp.int32, (n_rows, cap), 0)
    chosen, placing = lax.optimization_barrier((chosen.astype(BF16), placing.astype(BF16)))
    picked = jnp.dot(chosen, tokens, preferred_element_type=F32).astype(BF16)
    picked_grad = jnp.dot(chosen, cotangent, preferred_element_type=F32)
    scaled = (weighted * picked_grad).astype(BF16)
    picked_grad = picked_grad.astype(BF16)

    other = send(jnp.concatenate([picked, scaled], 0), CORE)
    lent = send(jnp.concatenate([picked[:part], scaled[:part]], 0), X_OUT)
    lent_back = send(jnp.concatenate([picked[part:], scaled[part:]], 0), X_BACK)
    guests = (lent, lent_back, send(lent, CORE), send(lent_back, CORE))
    rows = (
        jnp.concatenate([picked, other[:cap]], 0),
        jnp.concatenate([guest[:part] for guest in guests], 0),
    )
    grads = (
        jnp.concatenate([scaled, other[cap:]], 0),
        jnp.concatenate([guest[part:] for guest in guests], 0),
    )

    mats = by_matrix(ring)
    units = [forward(r, g, mats) for r, g in zip(rows, grads)]
    sides = ((0, rows), (1, rows), (2, grads))
    terms = [
        (inner_rows(units[0][i], side[0]) + inner_rows(units[1][i], side[1])).astype(BF16)
        for i, side in sides
    ]
    terms, units = lax.optimization_barrier((terms, units))
    guest_parts = [split_rows(t.astype(BF16), 4) for t in row_terms(units[1], mats)]
    guest_other = jnp.concatenate([p[i] for i in (2, 1) for p in guest_parts], 0)
    guest_own = jnp.concatenate([p[i] for i in (0, 3) for p in guest_parts], 0)
    guest_out = added(guest_own, send(guest_other, CORE))

    own, behind1, ahead1, behind2, ahead2, behind3, ahead3, far = by_piece(terms, len(ring))
    ahead3 = added(ahead3, send(far, Z_OUT))
    behind2 = added(behind2, send(behind3, Z_BACK))
    ahead2 = added(ahead2, send(ahead3, Z_OUT))
    behind1 = added(behind1, send(behind2, Z_BACK))
    ahead2, behind1, guest_out, units = lax.optimization_barrier(
        (ahead2, behind1, guest_out, units)
    )
    returned = send(guest_out, X_BACK)
    home = []
    for term in row_terms(units[0], mats):
        parts = split_rows(term.astype(BF16), 4)
        home.append([added(parts[k], send(parts[k + 2], CORE)) for k in range(2)])
    ahead1 = added(ahead1, send(ahead2, Z_OUT))
    total = own.astype(F32) + send(behind1, Z_BACK).astype(F32) + send(ahead1, Z_OUT).astype(F32)
    total = total.astype(BF16)
    quarter, returned = y_reduce(total, y, returned)

    others = send(returned, CORE)
    quarter = added(quarter, send(quarter, X_ACROSS))
    quarter, others = lax.optimization_barrier((quarter, others))
    total = placed(y_gather(quarter), y)
    returned, others = split_rows(returned, 4)[:2], split_rows(others, 4)[2:]
    expert_out, slot_grad = (
        jnp.concatenate([own[0].astype(F32) + low, own[1].astype(F32) + high], 0)
        for own, low, high in zip(home, returned, others)
    )
    gate_grad = live * jnp.sum(expert_out * picked_grad.astype(F32), axis=1)
    rows_out = ((weighted * expert_out).astype(BF16), slot_grad.astype(BF16))
    rows_out, gate_grad = lax.optimization_barrier((rows_out, gate_grad))
    layer_out, tokens_grad = (
        jnp.dot(placing, r, preferred_element_type=F32).astype(BF16) for r in rows_out
    )
    total, layer_out, tokens_grad, gate_grad = lax.optimization_barrier(
        (total, layer_out, tokens_grad, gate_grad)
    )
    swapped = send(total, CORE)
    first = jnp.where(core == 0, total, swapped)
    second = jnp.where(core == 0, swapped, total)
    g, u, d = (
        jnp.concatenate([first[i * half : (i + 1) * half], second[i * half : (i + 1) * half]], 0)
        for i in range(3)
    )
    return layer_out, tokens_grad, gate_grad, g.T, u.T, d


def solution(mesh):
    grid = Mesh(mesh.devices.reshape(2, NZ, 2, NY, 2), AXES)
    rows = P(AXES, None)
    vector = P(AXES)
    weights = (P(None, SHARD), P(None, SHARD), P(SHARD, None))
    return jax.shard_map(
        local,
        mesh=grid,
        in_specs=(rows, rows, vector, vector, vector) + weights,
        out_specs=(rows, rows, vector) + weights,
        check_vma=False,
    )
```

```python
import itertools

import jax
import jax.numpy as jnp
from jax import lax
from jax.sharding import Mesh, PartitionSpec as P

NX, NY, NZ = 4, 4, 8
AXES = ("xl", "z", "xh", "y", "c")
ROWS = P(AXES)
SHARD = ("xl", "z")
F32 = jnp.float32
BF16 = jnp.bfloat16


def device_index(x, y, z, c):
    return ((((x % 2) * NZ + z) * 2 + x // 2) * NY + y) * 2 + c


def route(move):
    pairs = []
    for x, y, z, c in itertools.product(range(NX), range(NY), range(NZ), range(2)):
        target = move(x, y, z, c)
        if target is None:
            continue
        tx, ty, tz, tc = target
        pairs.append((device_index(x, y, z, c), device_index(tx % NX, ty % NY, tz % NZ, tc)))
    return pairs


Z_OUT = route(lambda x, y, z, c: (x, y, z + 1 - 2 * c, c))
Z_BACK = route(lambda x, y, z, c: (x, y, z - 1 + 2 * c, c))
X_OUT = route(lambda x, y, z, c: (x + 1 - 2 * c, y, z, c))
X_BACK = route(lambda x, y, z, c: (x - 1 + 2 * c, y, z, c))
X_ACROSS = route(lambda x, y, z, c: (x + 2, y, z, c))
Y_UP = route(lambda x, y, z, c: (x, y + 1, z, c))
Y_DOWN = route(lambda x, y, z, c: (x, y - 1, z, c))
Y_TWO = route(lambda x, y, z, c: (x, y + 2, z, c))
CORE = route(lambda x, y, z, c: (x, y, z, 1 - c))


def send(block, pairs):
    return lax.ppermute(block, AXES, pairs)


def added(left, right):
    return (left.astype(F32) + right.astype(F32)).astype(BF16)


def columns(block, index, count):
    width = block.shape[-1] // count
    return lax.dynamic_slice_in_dim(block, (index % count) * width, width, block.ndim - 1)


def y_gather(block):
    return block, send(block, Y_UP), send(block, Y_DOWN), send(block, Y_TWO)


def placed(blocks, index):
    own, below, above, across = blocks
    width = own.shape[-1]
    whole = jnp.zeros(own.shape[:-1] + (4 * width,), own.dtype)
    for shift, part in ((0, own), (3, below), (1, above), (2, across)):
        start = ((index + shift) % 4) * width
        whole = lax.dynamic_update_slice_in_dim(whole, part, start, own.ndim - 1)
    return whole


def y_reduce(block, y, other):
    routes = ((1, Y_UP), (3, Y_DOWN), (2, Y_TWO))
    parts = [send(columns(block, y + shift, 4), pairs) for shift, pairs in routes]
    parts, other = lax.optimization_barrier((parts, other))
    total = columns(block, y, 4).astype(F32)
    for part in parts:
        total = total + part.astype(F32)
    return total.astype(BF16), other


def ring8_gather(block):
    blocks = [block]
    behind, ahead = block, block
    for _ in range(3):
        behind = send(behind, Z_OUT)
        ahead = send(ahead, Z_BACK)
        blocks += [behind, ahead]
    return blocks + [send(behind, Z_OUT)]


def inner_rows(left, right):
    return lax.dot_general(left, right, (((0,), (0,)), ((), ())), preferred_element_type=F32)


def inner_cols(left, right):
    return lax.dot_general(left, right, (((1,), (1,)), ((), ())), preferred_element_type=F32)


def split_rows(block, count):
    rows = block.shape[0] // count
    return [block[i * rows : (i + 1) * rows] for i in range(count)]


def by_matrix(pieces):
    width = pieces[0].shape[-1]
    whole = jnp.concatenate([p.reshape(3, -1, width) for p in pieces], 1)
    return whole[0], whole[1], whole[2]


def by_piece(terms, count):
    parts = [split_rows(term, count) for term in terms]
    return [jnp.concatenate([part[i] for part in parts], 0) for i in range(count)]


def forward(rows, scaled, mats):
    w_gate, w_up, w_down = mats
    gate_pre = inner_cols(rows, w_gate)
    up_pre = inner_cols(rows, w_up)
    hidden_grad = inner_cols(scaled, w_down)
    sigma = jax.nn.sigmoid(gate_pre)
    active = gate_pre * sigma
    hidden = (active * up_pre).astype(BF16)
    pre_gate = (hidden_grad * up_pre * (sigma + active * (1.0 - sigma))).astype(BF16)
    pre_up = (hidden_grad * active).astype(BF16)
    return pre_gate, pre_up, hidden


def row_terms(units, mats):
    pre_gate, pre_up, hidden = units
    w_gate, w_up, w_down = mats
    expert_part = jnp.dot(hidden, w_down, preferred_element_type=F32)
    slot_part = jnp.dot(pre_gate, w_gate, preferred_element_type=F32)
    return expert_part, slot_part + jnp.dot(pre_up, w_up, preferred_element_type=F32)


def local(
    tokens, cotangent, gate_values, slot_rows, slot_counts, gate_weight, up_weight, down_weight
):
    cap = slot_rows.shape[0]
    n_rows = tokens.shape[0]
    part = cap // 2
    y, core = lax.axis_index("y"), lax.axis_index("c")
    half = down_weight.shape[0] // 2

    mats = (gate_weight.T, up_weight.T, down_weight)
    piece = jnp.concatenate([lax.dynamic_slice_in_dim(m, core * half, half, 0) for m in mats], 0)
    ring = ring8_gather(piece)

    live = (lax.iota(jnp.int32, cap) < slot_counts[0]).astype(F32)
    weighted = (gate_values * live)[:, None]
    chosen = slot_rows[:, None] == lax.broadcasted_iota(jnp.int32, (cap, n_rows), 1)
    chosen = chosen.astype(BF16)
    picked = jnp.dot(chosen, tokens, preferred_element_type=F32).astype(BF16)
    picked_grad = jnp.dot(chosen, cotangent, preferred_element_type=F32)
    scaled = (weighted * picked_grad).astype(BF16)
    picked_grad = picked_grad.astype(BF16)

    other = send(jnp.concatenate([picked, scaled], 0), CORE)
    lent = send(jnp.concatenate([picked[:part], scaled[:part]], 0), X_OUT)
    lent_back = send(jnp.concatenate([picked[part:], scaled[part:]], 0), X_BACK)
    guests = (lent, lent_back, send(lent, CORE), send(lent_back, CORE))
    rows = (
        jnp.concatenate([picked, other[:cap]], 0),
        jnp.concatenate([guest[:part] for guest in guests], 0),
    )
    grads = (
        jnp.concatenate([scaled, other[cap:]], 0),
        jnp.concatenate([guest[part:] for guest in guests], 0),
    )

    mats = by_matrix(ring)
    units = [forward(r, g, mats) for r, g in zip(rows, grads)]
    sides = ((0, rows), (1, rows), (2, grads))
    terms = [
        (inner_rows(units[0][i], side[0]) + inner_rows(units[1][i], side[1])).astype(BF16)
        for i, side in sides
    ]
    terms, units = lax.optimization_barrier((terms, units))
    guest_out = []
    for term in row_terms(units[1], mats):
        parts = split_rows(term.astype(BF16), 4)
        guest_out.append([added(parts[k], send(parts[m], CORE)) for k, m in ((0, 2), (3, 1))])
    guest_out = jnp.concatenate([g[k] for k in range(2) for g in guest_out], 0)

    own, behind1, ahead1, behind2, ahead2, behind3, ahead3, far = by_piece(terms, len(ring))
    ahead3 = added(ahead3, send(far, Z_OUT))
    behind2 = added(behind2, send(behind3, Z_BACK))
    behind2, guest_out = lax.optimization_barrier((behind2, guest_out))
    returned = send(guest_out, X_BACK)
    ahead2 = added(ahead2, send(ahead3, Z_OUT))
    behind1 = added(behind1, send(behind2, Z_BACK))
    placing = slot_rows[None, :] == lax.broadcasted_iota(jnp.int32, (n_rows, cap), 0)
    behind1, units, placing = lax.optimization_barrier((behind1, units, placing.astype(BF16)))
    home = []
    for term in row_terms(units[0], mats):
        parts = split_rows(term.astype(BF16), 4)
        home.append([added(parts[k], send(parts[k + 2], CORE)) for k in range(2)])
    ahead1 = added(ahead1, send(ahead2, Z_OUT))
    total = own.astype(F32) + send(behind1, Z_BACK).astype(F32) + send(ahead1, Z_OUT).astype(F32)
    total = total.astype(BF16)
    quarter, returned = y_reduce(total, y, returned)

    others = send(returned, CORE)
    quarter = added(quarter, send(quarter, X_ACROSS))
    quarter, others = lax.optimization_barrier((quarter, others))
    total = placed(y_gather(quarter), y)
    returned, others = split_rows(returned, 4)[:2], split_rows(others, 4)[2:]
    expert_out, slot_grad = (
        jnp.concatenate([own[0].astype(F32) + low, own[1].astype(F32) + high], 0)
        for own, low, high in zip(home, returned, others)
    )
    gate_grad = live * jnp.sum(expert_out * picked_grad.astype(F32), axis=1)
    rows_out = ((weighted * expert_out).astype(BF16), slot_grad.astype(BF16))
    rows_out, gate_grad = lax.optimization_barrier((rows_out, gate_grad))
    layer_out, tokens_grad = (
        jnp.dot(placing, r, preferred_element_type=F32).astype(BF16) for r in rows_out
    )
    total, layer_out, tokens_grad, gate_grad = lax.optimization_barrier(
        (total, layer_out, tokens_grad, gate_grad)
    )
    swapped = send(total, CORE)
    first = jnp.where(core == 0, total, swapped)
    second = jnp.where(core == 0, swapped, total)
    g, u, d = (
        jnp.concatenate([first[i * half : (i + 1) * half], second[i * half : (i + 1) * half]], 0)
        for i in range(3)
    )
    return layer_out, tokens_grad, gate_grad, g.T, u.T, d


def solution(mesh):
    grid = Mesh(mesh.devices.reshape(2, NZ, 2, NY, 2), AXES)
    rows = P(AXES, None)
    vector = P(AXES)
    weights = (P(None, SHARD), P(None, SHARD), P(SHARD, None))
    return jax.shard_map(
        local,
        mesh=grid,
        in_specs=(rows, rows, vector, vector, vector) + weights,
        out_specs=(rows, rows, vector) + weights,
        check_vma=False,
    )
```

```python
import itertools

import jax
import jax.numpy as jnp
from jax import lax
from jax.sharding import Mesh, PartitionSpec as P

NX, NY, NZ = 4, 4, 8
AXES = ("xl", "z", "xh", "y", "c")
ROWS = P(AXES)
SHARD = ("xl", "z")
F32 = jnp.float32
BF16 = jnp.bfloat16


def device_index(x, y, z, c):
    return ((((x % 2) * NZ + z) * 2 + x // 2) * NY + y) * 2 + c


def route(move):
    pairs = []
    for x, y, z, c in itertools.product(range(NX), range(NY), range(NZ), range(2)):
        target = move(x, y, z, c)
        if target is None:
            continue
        tx, ty, tz, tc = target
        pairs.append((device_index(x, y, z, c), device_index(tx % NX, ty % NY, tz % NZ, tc)))
    return pairs


Z_OUT = route(lambda x, y, z, c: (x, y, z + 1 - 2 * c, c))
Z_BACK = route(lambda x, y, z, c: (x, y, z - 1 + 2 * c, c))
X_OUT = route(lambda x, y, z, c: (x + 1 - 2 * c, y, z, c))
X_BACK = route(lambda x, y, z, c: (x - 1 + 2 * c, y, z, c))
X_ACROSS = route(lambda x, y, z, c: (x + 2, y, z, c))
Y_UP = route(lambda x, y, z, c: (x, y + 1, z, c))
Y_DOWN = route(lambda x, y, z, c: (x, y - 1, z, c))
Y_TWO = route(lambda x, y, z, c: (x, y + 2, z, c))
CORE = route(lambda x, y, z, c: (x, y, z, 1 - c))


def send(block, pairs):
    return lax.ppermute(block, AXES, pairs)


def added(left, right):
    return (left.astype(F32) + right.astype(F32)).astype(BF16)


def columns(block, index, count):
    width = block.shape[-1] // count
    return lax.dynamic_slice_in_dim(block, (index % count) * width, width, block.ndim - 1)


def y_gather(block):
    return block, send(block, Y_UP), send(block, Y_DOWN), send(block, Y_TWO)


def placed(blocks, index):
    own, below, above, across = blocks
    width = own.shape[-1]
    whole = jnp.zeros(own.shape[:-1] + (4 * width,), own.dtype)
    for shift, part in ((0, own), (3, below), (1, above), (2, across)):
        start = ((index + shift) % 4) * width
        whole = lax.dynamic_update_slice_in_dim(whole, part, start, own.ndim - 1)
    return whole


def y_reduce(block, y, other):
    routes = ((1, Y_UP), (3, Y_DOWN), (2, Y_TWO))
    parts = [send(columns(block, y + shift, 4), pairs) for shift, pairs in routes]
    parts, other = lax.optimization_barrier((parts, other))
    total = columns(block, y, 4).astype(F32)
    for part in parts:
        total = total + part.astype(F32)
    return total.astype(BF16), other


def ring8_gather(block):
    blocks = [block]
    behind, ahead = block, block
    for _ in range(3):
        behind = send(behind, Z_OUT)
        ahead = send(ahead, Z_BACK)
        blocks += [behind, ahead]
    return blocks + [send(behind, Z_OUT)]


def inner_rows(left, right):
    return lax.dot_general(left, right, (((0,), (0,)), ((), ())), preferred_element_type=F32)


def inner_cols(left, right):
    return lax.dot_general(left, right, (((1,), (1,)), ((), ())), preferred_element_type=F32)


def split_rows(block, count):
    rows = block.shape[0] // count
    return [block[i * rows : (i + 1) * rows] for i in range(count)]


def by_matrix(pieces):
    width = pieces[0].shape[-1]
    whole = jnp.concatenate([p.reshape(3, -1, width) for p in pieces], 1)
    return whole[0], whole[1], whole[2]


def by_piece(terms, count):
    parts = [split_rows(term, count) for term in terms]
    return [jnp.concatenate([part[i] for part in parts], 0) for i in range(count)]


def forward(rows, scaled, mats):
    w_gate, w_up, w_down = mats
    gate_pre = inner_cols(rows, w_gate)
    up_pre = inner_cols(rows, w_up)
    hidden_grad = inner_cols(scaled, w_down)
    sigma = jax.nn.sigmoid(gate_pre)
    active = gate_pre * sigma
    hidden = (active * up_pre).astype(BF16)
    pre_gate = (hidden_grad * up_pre * (sigma + active * (1.0 - sigma))).astype(BF16)
    pre_up = (hidden_grad * active).astype(BF16)
    return pre_gate, pre_up, hidden


def row_terms(units, mats):
    pre_gate, pre_up, hidden = units
    w_gate, w_up, w_down = mats
    expert_part = jnp.dot(hidden, w_down, preferred_element_type=F32)
    slot_part = jnp.dot(pre_gate, w_gate, preferred_element_type=F32)
    return expert_part, slot_part + jnp.dot(pre_up, w_up, preferred_element_type=F32)


def local(
    tokens, cotangent, gate_values, slot_rows, slot_counts, gate_weight, up_weight, down_weight
):
    cap = slot_rows.shape[0]
    n_rows = tokens.shape[0]
    part = cap // 2
    y, core = lax.axis_index("y"), lax.axis_index("c")
    half = down_weight.shape[0] // 2

    mats = (gate_weight.T, up_weight.T, down_weight)
    piece = jnp.concatenate([lax.dynamic_slice_in_dim(m, core * half, half, 0) for m in mats], 0)
    ring = ring8_gather(piece)

    live = (lax.iota(jnp.int32, cap) < slot_counts[0]).astype(F32)
    weighted = (gate_values * live)[:, None]
    chosen = slot_rows[:, None] == lax.broadcasted_iota(jnp.int32, (cap, n_rows), 1)
    chosen = chosen.astype(BF16)
    picked = jnp.dot(chosen, tokens, preferred_element_type=F32).astype(BF16)
    picked_grad = jnp.dot(chosen, cotangent, preferred_element_type=F32)
    scaled = (weighted * picked_grad).astype(BF16)
    picked_grad = picked_grad.astype(BF16)

    other = send(jnp.concatenate([picked, scaled], 0), CORE)
    lent = send(jnp.concatenate([picked[:part], scaled[:part]], 0), X_OUT)
    lent_back = send(jnp.concatenate([picked[part:], scaled[part:]], 0), X_BACK)
    guests = (lent, lent_back, send(lent, CORE), send(lent_back, CORE))
    rows = (
        jnp.concatenate([picked, other[:cap]], 0),
        jnp.concatenate([guest[:part] for guest in guests], 0),
    )
    grads = (
        jnp.concatenate([scaled, other[cap:]], 0),
        jnp.concatenate([guest[part:] for guest in guests], 0),
    )

    mats = by_matrix(ring)
    units = [forward(r, g, mats) for r, g in zip(rows, grads)]
    sides = ((0, rows), (1, rows), (2, grads))
    terms = [
        (inner_rows(units[0][i], side[0]) + inner_rows(units[1][i], side[1])).astype(BF16)
        for i, side in sides
    ]
    terms, units = lax.optimization_barrier((terms, units))
    guest_out = []
    for term in row_terms(units[1], mats):
        parts = split_rows(term.astype(BF16), 4)
        guest_out.append([added(parts[k], send(parts[m], CORE)) for k, m in ((0, 2), (3, 1))])
    guest_out = jnp.concatenate([g[k] for k in range(2) for g in guest_out], 0)

    own, behind1, ahead1, behind2, ahead2, behind3, ahead3, far = by_piece(terms, len(ring))
    ahead3 = added(ahead3, send(far, Z_OUT))
    behind2 = added(behind2, send(behind3, Z_BACK))
    behind2, guest_out = lax.optimization_barrier((behind2, guest_out))
    returned = send(guest_out, X_BACK)
    ahead2 = added(ahead2, send(ahead3, Z_OUT))
    behind1 = added(behind1, send(behind2, Z_BACK))
    placing = slot_rows[None, :] == lax.broadcasted_iota(jnp.int32, (n_rows, cap), 0)
    behind1, units, placing = lax.optimization_barrier((behind1, units, placing.astype(BF16)))
    home = []
    for term in row_terms(units[0], mats):
        parts = split_rows(term.astype(BF16), 4)
        home.append([added(parts[k], send(parts[k + 2], CORE)) for k in range(2)])
    ahead1 = added(ahead1, send(ahead2, Z_OUT))
    total = own.astype(F32) + send(behind1, Z_BACK).astype(F32) + send(ahead1, Z_OUT).astype(F32)
    total = total.astype(BF16)
    quarter, (returned, home) = y_reduce(total, y, (returned, home))

    others = send(returned, CORE)
    quarter = added(quarter, send(quarter, X_ACROSS))
    quarter, others = lax.optimization_barrier((quarter, others))
    total = placed(y_gather(quarter), y)
    returned, others = split_rows(returned, 4)[:2], split_rows(others, 4)[2:]
    expert_out, slot_grad = (
        jnp.concatenate([own[0].astype(F32) + low, own[1].astype(F32) + high], 0)
        for own, low, high in zip(home, returned, others)
    )
    gate_grad = live * jnp.sum(expert_out * picked_grad.astype(F32), axis=1)
    rows_out = ((weighted * expert_out).astype(BF16), slot_grad.astype(BF16))
    rows_out, gate_grad = lax.optimization_barrier((rows_out, gate_grad))
    layer_out, tokens_grad = (
        jnp.dot(placing, r, preferred_element_type=F32).astype(BF16) for r in rows_out
    )
    total, layer_out, tokens_grad, gate_grad = lax.optimization_barrier(
        (total, layer_out, tokens_grad, gate_grad)
    )
    swapped = send(total, CORE)
    first = jnp.where(core == 0, total, swapped)
    second = jnp.where(core == 0, swapped, total)
    g, u, d = (
        jnp.concatenate([first[i * half : (i + 1) * half], second[i * half : (i + 1) * half]], 0)
        for i in range(3)
    )
    return layer_out, tokens_grad, gate_grad, g.T, u.T, d


def solution(mesh):
    grid = Mesh(mesh.devices.reshape(2, NZ, 2, NY, 2), AXES)
    rows = P(AXES, None)
    vector = P(AXES)
    weights = (P(None, SHARD), P(None, SHARD), P(SHARD, None))
    return jax.shard_map(
        local,
        mesh=grid,
        in_specs=(rows, rows, vector, vector, vector) + weights,
        out_specs=(rows, rows, vector) + weights,
        check_vma=False,
    )
```
